32 devices in a mesh: frag: 1, aux: 32 (over z, y, x, core), occ: 1.
Axes of the slice: x: 2, y: 2, z: 4, core: 2. Of those that a mesh axis runs over, the one named last changes fastest.
Arguments:
- integrals: bfloat16 [1280, 4, 128, 128], P(('frag', 'aux')), may hold values from -1 to 1
- block_list: int32 [1280, 3], P(('frag', 'aux')), may hold values from 0 to 1023, as said below
- block_count: int32 [32], P(('frag', 'aux')), may hold values from 30 to 40, as said below
- coeffs: bfloat16 [768, 128], P('frag', 'occ'), may hold values from -6 to 6
Outputs:
- exchange_matrix: float32 [768, 768], P(('frag', 'aux', 'occ'))
The draws below stay inside these ranges and needn't reach their ends.
Inputs may be any that keep to these rules, and one draw needn't show every extreme that they name: block_list[r] = (a, u, v) with a < 1024 and u, v < 6. Auxiliary block a belongs to slab a // 32. Among the live rows of one slab at most 2 name auxiliary blocks of one slab, and in every draw some slab receives exactly 2 from every slab. Rows past a slab's count hold valid indices but are not used. `block_count`: live rows come first on each slab; some slab is full in every draw.
All inputs are finite; a program needn't handle non-finite values.
Results may differ from the reference program's by a relative error of at most 0.0003.
Values may be sent and summed in bfloat16 or wider, within the bound.
A program may use at most 128 MiB of HBM per device.

```python
import math
import jax
import jax.numpy as jnp
from jax import lax

BS = 128
ABLK = 4
AUX_DEV = 128
OCC = 128
NB = 6
NNZ_DEV = 40
NAUX = 4096
NAB = 1024
NBAS = 768
CAP = 2
ROWS = 1280


def draw_block_list(key, part):
    key = jax.random.fold_in(key, 11)
    slab_count = NAUX // AUX_DEV
    owned_blocks = AUX_DEV // ABLK
    hot_slab = jax.random.randint(jax.random.fold_in(key, 1), (), 0, slab_count).astype(jnp.int32)
    spare_slots = (slab_count - 1) * CAP
    always_live = NNZ_DEV - NNZ_DEV // 4

    def one_device(slab_index):
        dev_key = jax.random.fold_in(key, slab_index + 7)
        first_key, second_key, third_key, fourth_key, fifth_key = jax.random.split(dev_key, 5)
        base_owner = jnp.arange(spare_slots, dtype=jnp.int32) // CAP
        other_owners = base_owner + (base_owner >= hot_slab).astype(jnp.int32)
        other_owners = jax.random.permutation(first_key, other_owners)[:NNZ_DEV - CAP]
        owners = jnp.concatenate([jnp.full((CAP,), 1, jnp.int32) * hot_slab, other_owners])
        shuffle = jax.random.permutation(second_key, always_live)
        owners = jnp.concatenate([owners[:always_live][shuffle], owners[always_live:]])
        local_block = jax.random.randint(third_key, (NNZ_DEV,), 0, owned_blocks).astype(jnp.int32)
        top_row = jnp.argmax(owners).astype(jnp.int32)
        row_ids = jnp.arange(NNZ_DEV, dtype=jnp.int32)
        local_block = jnp.where(row_ids == top_row, owned_blocks - 1, local_block).astype(jnp.int32)
        row_block = jax.random.randint(fourth_key, (NNZ_DEV,), 0, NB).astype(jnp.int32)
        col_block = jax.random.randint(fifth_key, (NNZ_DEV,), 0, NB).astype(jnp.int32)
        col_block = jnp.where((row_ids == 0) & (slab_index == 0), 0, col_block).astype(jnp.int32)
        return jnp.stack([owners * owned_blocks + local_block, row_block, col_block], axis=1)
    all_rows = jax.vmap(one_device)(jnp.arange(slab_count, dtype=jnp.int32))
    return all_rows.reshape(slab_count * NNZ_DEV, 3)


def draw_block_count(key, part):
    key = jax.random.fold_in(key, 23)
    slab_count = NAUX // AUX_DEV
    least_count = NNZ_DEV - NNZ_DEV // 4
    first_key, second_key, third_key = jax.random.split(key, 3)
    live_counts = jax.random.randint(first_key, (slab_count,), least_count, NNZ_DEV + 1).astype(jnp.int32)
    full_slab = jax.random.randint(second_key, (), 0, slab_count)
    least_slab = (full_slab + 1 + jax.random.randint(third_key, (), 0, slab_count - 1)) % slab_count
    slab_ids = jnp.arange(slab_count, dtype=jnp.int32)
    live_counts = jnp.where(slab_ids == full_slab, NNZ_DEV, live_counts)
    live_counts = jnp.where(slab_ids == least_slab, least_count, live_counts)
    return live_counts.astype(jnp.int32)


def draw_integrals(key, part):
    key = jax.random.fold_in(key, 31)
    noise_key, height_key, freq_key, phase_key = jax.random.split(key, 4)
    sigma = float(BS) ** (-0.5)
    full_shape = (ROWS, ABLK, BS, BS)
    wave_shape = (ROWS, ABLK, 1, BS)
    noise = jnp.clip(jax.random.normal(noise_key, full_shape, jnp.float32), -4.0, 4.0)
    height = jax.random.uniform(height_key, wave_shape, jnp.float32, 0.5, 1.5)
    offset = 1.2
    freq = jax.random.uniform(freq_key, wave_shape, jnp.float32, 0.0, 6.0 * math.pi / BS)
    phase = jax.random.uniform(phase_key, wave_shape, jnp.float32, -math.pi, math.pi)
    basis_rows = jnp.arange(BS, dtype=jnp.float32)[None, None, :, None]
    common = height * (offset * sigma + jnp.cos(freq * basis_rows + phase))
    return jnp.clip(sigma * (noise + common), -1.0, 1.0).astype(jnp.bfloat16)


def signed_parity(row_index, col_index):
    shared = jnp.zeros(row_index.shape[:-1] + (row_index.shape[-1], col_index.shape[-1]), jnp.int32)
    for bit_place in range(16):
        row_bit = row_index // 2 ** bit_place % 2
        col_bit = col_index // 2 ** bit_place % 2
        shared = shared + row_bit[..., :, None] * col_bit[..., None, :]
    return (1 - 2 * (shared % 2)).astype(jnp.float32)


def draw_coeffs(key, part):
    key = jax.random.fold_in(key, 37)
    noise_key, level_key, sign_key, scale_key, row_key, col_key, rsign_key, csign_key = jax.random.split(key, 8)
    noise = 0.35 * jnp.clip(jax.random.normal(noise_key, (NBAS, OCC), jnp.float32), -4.0, 4.0)
    block_scale = jnp.exp(jax.random.uniform(scale_key, (NB, 1, 1), jnp.float32, math.log(0.8), math.log(1.25)))
    level = jax.random.uniform(level_key, (OCC,), jnp.float32, 0.15, 0.35)
    row_order = jax.vmap(lambda k: jax.random.permutation(k, BS))(jax.random.split(row_key, NB)).astype(jnp.int32)
    col_order = jax.vmap(lambda k: jax.random.permutation(k, OCC))(jax.random.split(col_key, NB)).astype(jnp.int32)
    pattern = signed_parity(row_order, col_order)
    row_sign = jnp.where(jax.random.bernoulli(rsign_key, 0.5, (NB, BS, 1)), 1.0, -1.0).astype(jnp.float32)
    col_sign = jnp.where(jax.random.bernoulli(csign_key, 0.5, (NB, 1, OCC)), 1.0, -1.0).astype(jnp.float32)
    flat = (1.3 * block_scale * row_sign * col_sign * pattern).reshape(NBAS, OCC)
    signs = jnp.where(jax.random.bernoulli(sign_key, 0.5, (OCC,)), 1.0, -1.0).astype(jnp.float32)
    return jnp.clip(flat + noise + (signs * level)[None, :], -6.0, 6.0).astype(jnp.bfloat16)


def setup_inputs(seed: int = 0, part: int = 0) -> dict:
    keys = jax.random.split(jax.random.key(seed), 5)
    part_splits = jax.random.split(jax.random.fold_in(keys[4], part), 5)
    return {
        "integrals": draw_integrals(jax.random.fold_in(jax.random.fold_in(keys[4], part), 71), part),
        "block_list": draw_block_list(jax.random.fold_in(jax.random.fold_in(keys[4], part), 71), part),
        "block_count": draw_block_count(jax.random.fold_in(jax.random.fold_in(keys[4], part), 71), part),
        "coeffs": draw_coeffs(jax.random.fold_in(jax.random.fold_in(keys[4], part), 71), part),
    }


def reference(integrals, block_list, block_count, coeffs):
    slab_count = NAUX // AUX_DEV
    owned_blocks = NAB // slab_count
    coef_blocks = coeffs.reshape(NB, BS, OCC)
    segments = NAB * NB

    def add_slab(fitted, slab_index):
        slab_ints = lax.dynamic_slice_in_dim(integrals, slab_index * NNZ_DEV, NNZ_DEV, 0)
        slab_tags = lax.dynamic_slice_in_dim(block_list, slab_index * NNZ_DEV, NNZ_DEV, 0)
        is_live = jnp.arange(NNZ_DEV, dtype=jnp.int32) < block_count[slab_index]
        picked = coef_blocks[slab_tags[:, 2]]
        half_rows = jnp.einsum("bpml,blo->bpmo", slab_ints.astype(jnp.float32), picked.astype(jnp.float32)).astype(jnp.bfloat16)
        seg_index = jnp.where(is_live, slab_tags[:, 0] * NB + slab_tags[:, 1], segments).astype(jnp.int32)
        return fitted.at[seg_index].add(half_rows.astype(jnp.float32), mode="drop"), None

    start_fit = jnp.zeros((segments, ABLK, BS, OCC), jnp.float32)
    fitted, _ = lax.scan(add_slab, start_fit, jnp.arange(slab_count, dtype=jnp.int32))
    fitted = fitted.astype(jnp.bfloat16).reshape(slab_count, owned_blocks, NB, ABLK, BS, OCC)

    def add_product(running, slab_block):
        flat_rows = slab_block.transpose(1, 3, 0, 2, 4).reshape(NBAS, owned_blocks * ABLK * OCC)
        return running + jnp.dot(flat_rows, flat_rows.T, preferred_element_type=jnp.float32), None

    running, _ = lax.scan(add_product, jnp.zeros((NBAS, NBAS), jnp.float32), fitted)
    return running / (NAUX * OCC)
```

```python
import functools

import jax
import jax.numpy as jnp
from jax import lax
from jax.experimental import pallas as pl
from jax.experimental.pallas import tpu as pltpu
from jax.sharding import PartitionSpec as P

AUX_DEV = 128
OCC = 128
MESH = pl.DeviceIdType.MESH
NT = (((1,), (1,)), ((), ()))


def send_half_blocks(nodes, slots, source, vblock, tags, integrals, coeffs, recv, recv_tags,
                     half, send_sem, recv_sem, tag_send, tag_recv, own_sem):
    me = lax.axis_index("aux")
    barrier = pltpu.get_barrier_semaphore()

    @pl.loop(1, nodes)
    def _(k):
        pl.semaphore_signal(
            barrier, inc=1, device_id={"aux": lax.rem(me + k, nodes)}, device_id_type=MESH
        )

    def fill(peer):
        for s in range(slots):
            block = integrals[source[peer, s]]
            panel = coeffs[vblock[peer, s]]
            aux_width, size, inner = block.shape
            out = jnp.dot(
                block.reshape(aux_width * size, inner), panel, preferred_element_type=jnp.float32
            )
            half[peer, s] = out.astype(jnp.bfloat16).reshape(aux_width, size, panel.shape[1])

    def order(i):
        return nodes // 2 + (i + 1) // 2 * (1 - 2 * (i % 2))

    def copies(i):
        k = order(i)
        peer = lax.rem(me + k, nodes)
        data = pltpu.make_async_remote_copy(
            src_ref=half.at[peer], dst_ref=recv.at[me], send_sem=send_sem.at[k],
            recv_sem=recv_sem.at[k], device_id={"aux": peer}, device_id_type=MESH,
        )
        tag = pltpu.make_async_remote_copy(
            src_ref=tags.at[peer], dst_ref=recv_tags.at[me], send_sem=tag_send.at[k],
            recv_sem=tag_recv.at[k], device_id={"aux": peer}, device_id_type=MESH,
        )
        return data, tag

    fill(lax.rem(me + nodes // 2, nodes))
    pl.semaphore_wait(barrier, nodes - 1)

    @pl.loop(0, nodes - 1)
    def _(i):
        data, tag = copies(i)
        data.start()
        tag.start()
        later = jnp.where(i == nodes - 2, 0, order(i + 1))
        fill(lax.rem(me + later, nodes))

    own = pltpu.make_async_copy(half.at[me], recv.at[me], own_sem.at[0])
    own_tag = pltpu.make_async_copy(tags.at[me], recv_tags.at[me], own_sem.at[1])
    own.start()
    own_tag.start()
    own.wait()
    own_tag.wait()

    @pl.loop(0, nodes - 1)
    def _(i):
        data, tag = copies(i)
        data.wait()
        tag.wait()


def gram(scale, slots, tags, recv, out, total, fitted, head, following, count, mask):
    nodes, _, aux_width, size, occ = recv.shape
    owned = head.shape[0]
    wide = 2 * size
    groups = out.shape[0] // wide
    out[...] = jnp.zeros_like(out)

    @pl.loop(0, owned)
    def _(a):
        head[a] = 0
        count[a] = 0
        mask[a] = 0

    @pl.loop(0, nodes)
    def _(node):
        for s in range(slots):
            a = tags[node, 2 * s]
            u = tags[node, 2 * s + 1]

            @pl.when(u >= 0)
            def _():
                item = node * slots + s
                following[item] = head[a]
                head[a] = item
                count[a] = count[a] + 1
                mask[a] = mask[a] | (1 << (u // 2))

    @pl.loop(0, owned)
    def _(a):
        bits = mask[a]
        here = [((bits >> i) & 1) == 1 for i in range(groups)]
        spans = [pl.ds(i * wide, wide) for i in range(groups)]

        @pl.when(bits != 0)
        def _():
            for i in range(groups):
                @pl.when(here[i])
                def _():
                    total[spans[i], :] = jnp.zeros((wide, total.shape[1]), jnp.float32)

            def add(_, item):
                node, s = item // slots, item % slots
                u = tags[node, 2 * s + 1]
                rows = pl.ds(pl.multiple_of(u * size, size), size)
                for p in range(aux_width):
                    total[rows, pl.ds(p * occ, occ)] += recv[node, s, p].astype(jnp.float32)
                return following[item]

            lax.fori_loop(0, count[a], add, head[a])
            for i in range(groups):
                @pl.when(here[i])
                def _():
                    fitted[spans[i], :] = total[spans[i], :].astype(jnp.bfloat16)
            for i in range(groups):
                for j in range(groups):
                    @pl.when(here[i] & here[j])
                    def _():
                        out[spans[i], spans[j]] += lax.dot_general(
                            fitted[spans[i], :], fitted[spans[j], :], NT,
                            preferred_element_type=jnp.float32,
                        )

    out[...] = out[...] * scale


def exchange(buf, cols, dims, name, coords, sizes, rank_of, landing, send_sem, recv_sem):
    at = dims.index(name)
    found = []
    for step in range(1, sizes[name]):
        other = lax.rem(coords[name] + step, sizes[name])
        target = dict(coords)
        target[name] = other
        pick = (slice(None),) * at + (other,) + (slice(None),) * (len(dims) - at - 1)
        found.append(
            pltpu.make_async_remote_copy(
                src_ref=buf.at[pick + (slice(None), cols)], dst_ref=landing.at[step - 1],
                send_sem=send_sem.at[step - 1], recv_sem=recv_sem.at[step - 1],
                device_id={"aux": rank_of(target)}, device_id_type=MESH,
            )
        )
    return found


def gathered(buf, cols, dims, name, coords, landing, copies):
    at = dims.index(name)
    pick = (slice(None),) * at + (coords[name],) + (slice(None),) * (len(dims) - at - 1)
    value = buf[pick + (slice(None), cols)]
    for step, copy in enumerate(copies):
        copy.wait()
        value = value + landing[step]
    return value


ORDERS = (("x", "y", "z"), ("y", "z", "x"), ("z", "x", "y"))


def scatter_sum(sizes, part, *refs):
    own, out, first, landed = refs[:4]
    lands = refs[4:13]
    held = refs[13:19]
    send_sem, recv_sem = refs[19:]
    me = lax.axis_index("aux")
    names = ("z", "y", "x", "c")
    coords = {
        "c": me % 2, "x": me // 2 % 2, "y": me // 4 % 2, "z": me // 8,
    }

    def rank_of(c):
        return ((c["z"] * sizes["y"] + c["y"]) * sizes["x"] + c["x"]) * sizes["c"] + c["c"]

    barrier = pltpu.get_barrier_semaphore()
    partners = 0
    for name in names:
        for step in range(1, sizes[name]):
            target = dict(coords)
            target[name] = lax.rem(coords[name] + step, sizes[name])
            pl.semaphore_signal(
                barrier, inc=1, device_id={"aux": rank_of(target)}, device_id_type=MESH
            )
            partners += 1
    pl.semaphore_wait(barrier, partners)

    everything = slice(None)
    copies = exchange(own, everything, names, "c", coords, sizes, rank_of, landed,
                      send_sem.at[9], recv_sem.at[9])
    for copy in copies:
        copy.start()
    first[...] = gathered(own, everything, names, "c", coords, landed, copies)
    bufs = [first] * 3
    left = [list(names[:3]) for _ in range(3)]
    for stage in range(3):
        running = []
        for p in range(3):
            cols = pl.ds(p * part, part) if stage == 0 else slice(None)
            lane = stage * 3 + p
            copies = exchange(bufs[p], cols, left[p], ORDERS[p][stage], coords, sizes, rank_of,
                              lands[lane], send_sem.at[lane], recv_sem.at[lane])
            for copy in copies:
                copy.start()
            running.append((cols, copies))
        for p in range(3):
            cols, copies = running[p]
            value = gathered(bufs[p], cols, left[p], ORDERS[p][stage], coords,
                             lands[stage * 3 + p], copies)
            if stage == 2:
                out[:, pl.ds(p * part, part)] = value
            else:
                bufs[p] = held[stage * 3 + p]
                bufs[p][...] = value
            left[p].remove(ORDERS[p][stage])


def reduce_scatter(matrix, nodes):
    rows, columns = matrix.shape
    sizes = {"z": nodes // 8, "y": 2, "x": 2, "c": 2}
    height, part = rows // nodes, columns // 3
    deepest = max(sizes["z"] - 1, 1)
    lands, held = [], []
    for stage in range(3):
        for p in range(3):
            rest = tuple(sizes[d] for d in ("z", "y", "x") if d not in ORDERS[p][: stage + 1])
            shape = rest + (height, part)
            lands.append(pltpu.VMEM((sizes[ORDERS[p][stage]] - 1,) + shape, jnp.float32))
            if stage < 2:
                held.append(pltpu.VMEM(shape, jnp.float32))
    half = (sizes["z"], 2, 2, height, columns)
    return pl.pallas_call(
        functools.partial(scatter_sum, sizes, part),
        out_shape=jax.ShapeDtypeStruct((height, columns), jnp.float32),
        in_specs=[pl.BlockSpec(memory_space=pltpu.VMEM)],
        out_specs=pl.BlockSpec(memory_space=pltpu.VMEM),
        scratch_shapes=[
            pltpu.VMEM(half, jnp.float32),
            pltpu.VMEM((1,) + half, jnp.float32),
            *lands,
            *held,
            pltpu.SemaphoreType.DMA((10, deepest)),
            pltpu.SemaphoreType.DMA((10, deepest)),
        ],
        compiler_params=pltpu.CompilerParams(
            collective_id=1, has_side_effects=True, vmem_limit_bytes=40 * 2**20
        ),
    )(matrix.reshape(sizes["z"], 2, 2, 2, height, columns))


def fused_body(integrals, block_list, block_count, coeffs):
    stored, aux_width, size, _ = integrals.shape
    basis, occ = coeffs.shape
    nodes = lax.axis_size("aux")
    owned = AUX_DEV // aux_width
    slots = max(2, 64 // nodes)
    positions = jnp.arange(stored, dtype=jnp.int32)
    owner = jnp.where(positions < block_count[0], block_list[:, 0] // owned, nodes)
    before = (owner[:, None] == owner[None, :]) & (positions[None, :] < positions[:, None])
    target = owner * slots + jnp.sum(before.astype(jnp.int32), axis=1)
    chosen = (target[None, :] == jnp.arange(nodes * slots, dtype=jnp.int32)[:, None]).astype(
        jnp.int32
    )
    fields = jnp.stack(
        [positions, block_list[:, 2], block_list[:, 0] % owned, block_list[:, 1] + 1], axis=0
    )
    picked = jnp.sum(chosen[None] * fields[:, None, :], axis=2)
    source = picked[0].reshape(nodes, slots)
    vblock = picked[1].reshape(nodes, slots)
    tags = jnp.stack([picked[2], picked[3] - 1], axis=1).reshape(nodes, 1, 2 * slots)
    tags = jnp.pad(tags, ((0, 0), (0, 0), (0, 128 - 2 * slots)))
    vmem = pl.BlockSpec(memory_space=pltpu.VMEM)
    smem = pl.BlockSpec(memory_space=pltpu.SMEM)
    recv, recv_tags = pl.pallas_call(
        functools.partial(send_half_blocks, nodes, slots),
        out_shape=(
            jax.ShapeDtypeStruct((nodes, slots, aux_width, size, occ), jnp.bfloat16),
            jax.ShapeDtypeStruct((nodes, 1, 128), jnp.int32),
        ),
        in_specs=[smem, smem, vmem, vmem, vmem],
        out_specs=(pl.BlockSpec(memory_space=pl.ANY), vmem),
        scratch_shapes=[
            pltpu.VMEM((nodes, slots, aux_width, size, occ), jnp.bfloat16),
            pltpu.SemaphoreType.DMA((nodes,)),
            pltpu.SemaphoreType.DMA((nodes,)),
            pltpu.SemaphoreType.DMA((nodes,)),
            pltpu.SemaphoreType.DMA((nodes,)),
            pltpu.SemaphoreType.DMA((2,)),
        ],
        compiler_params=pltpu.CompilerParams(
            collective_id=0, has_side_effects=True, vmem_limit_bytes=40 * 2**20
        ),
    )(source, vblock, tags, integrals, coeffs.reshape(basis // size, size, occ))
    matrix = pl.pallas_call(
        functools.partial(gram, 1.0 / (AUX_DEV * nodes * OCC), slots),
        out_shape=jax.ShapeDtypeStruct((basis, basis), jnp.float32),
        in_specs=[smem, vmem],
        out_specs=vmem,
        scratch_shapes=[
            pltpu.VMEM((basis, aux_width * occ), jnp.float32),
            pltpu.VMEM((basis, aux_width * occ), jnp.bfloat16),
            pltpu.SMEM((owned,), jnp.int32),
            pltpu.SMEM((nodes * slots,), jnp.int32),
            pltpu.SMEM((owned,), jnp.int32),
            pltpu.SMEM((owned,), jnp.int32),
        ],
        compiler_params=pltpu.CompilerParams(vmem_limit_bytes=40 * 2**20),
    )(recv_tags.reshape(nodes, 128), recv)
    return reduce_scatter(matrix, nodes)


def body(integrals, block_list, block_count, coeffs):
    stored, aux_width, block_size, _ = integrals.shape
    basis, occ_local = coeffs.shape
    basis_blocks = basis // block_size
    aux_nodes = lax.axis_size("aux")
    owned_blocks = AUX_DEV // aux_width
    slot_count = max(2, 64 // aux_nodes)
    segments = owned_blocks * basis_blocks
    coef_blocks = coeffs.reshape(basis_blocks, block_size, occ_local)
    positions = jnp.arange(stored, dtype=jnp.int32)
    is_live = positions < block_count[0]
    owner_slab = jnp.where(is_live, block_list[:, 0] // owned_blocks, aux_nodes)
    member = (owner_slab[:, None] == jnp.arange(aux_nodes, dtype=jnp.int32)[None, :]).astype(
        jnp.int32
    )
    earlier = jnp.cumsum(member, axis=0) - member
    placed = jnp.sum(earlier * member, axis=1)
    target = jnp.where(is_live, owner_slab * slot_count + placed, aux_nodes * slot_count)
    source = (
        jnp.full((aux_nodes * slot_count + 1,), stored, jnp.int32)
        .at[target]
        .set(positions)[: aux_nodes * slot_count]
    )
    blank_tag = jnp.full((1, 3), -1, jnp.int32)
    send_tags = jnp.concatenate([block_list, blank_tag], axis=0)[source].reshape(
        aux_nodes, slot_count, 3
    )
    recv_tags = lax.all_to_all(send_tags, "aux", split_axis=0, concat_axis=0, tiled=True).reshape(
        aux_nodes * slot_count, 3
    )
    filled = recv_tags[:, 1] >= 0
    seg_of = jnp.where(
        filled, recv_tags[:, 1] * owned_blocks + recv_tags[:, 0] % owned_blocks, segments
    )
    seg_table = (jnp.arange(segments, dtype=jnp.int32)[:, None] == seg_of[None, :]).astype(
        jnp.bfloat16
    )
    padded = jnp.concatenate(
        [integrals, jnp.zeros((1,) + integrals.shape[1:], jnp.bfloat16)], axis=0
    )
    outgoing = padded[source].reshape(aux_nodes, slot_count, aux_width, block_size, block_size)
    lam_index = jnp.where(filled, recv_tags[:, 2], 0)
    recv_coef = coef_blocks[lam_index]
    item_block = lax.all_to_all(outgoing, "aux", split_axis=0, concat_axis=0, tiled=True)
    item_count = item_block.shape[2]
    flat_ints = item_block.reshape(aux_nodes * slot_count, item_count, block_size, block_size)
    half_rows = lax.dot_general(
        flat_ints, recv_coef, (((3,), (1,)), ((0,), (0,))), preferred_element_type=jnp.float32
    ).astype(jnp.bfloat16)
    summed = jnp.dot(
        seg_table, half_rows.reshape(aux_nodes * slot_count, -1), preferred_element_type=jnp.float32
    )
    fitted = summed.reshape(segments, item_count, block_size, occ_local)
    fitted = fitted.astype(jnp.bfloat16).reshape(
        basis_blocks, owned_blocks, aux_width, block_size, occ_local
    )
    fitted = fitted.transpose(0, 3, 1, 2, 4).reshape(basis, owned_blocks * aux_width * occ_local)
    scale_factor = 1.0 / (AUX_DEV * aux_nodes * OCC)
    return lax.psum_scatter(
        lax.dot_general(
            fitted, fitted, (((1,), (1,)), ((), ())), preferred_element_type=jnp.float32
        )
        * scale_factor,
        ("aux", "occ"),
        scatter_dimension=0,
        tiled=True,
    )


def solution(mesh):
    placed = (
        P(("frag", "aux"), None, None, None),
        P(("frag", "aux"), None),
        P(("frag", "aux")),
        P("frag", "occ"),
    )
    simple = mesh.shape["occ"] == 1 and mesh.shape["aux"] % 8 == 0
    return jax.shard_map(
        fused_body if simple else body, mesh=mesh, in_specs=placed, out_specs=P(("frag", "aux", "occ"), None), check_vma=False
    )
```

```python
import functools

import jax
import jax.numpy as jnp
from jax import lax
from jax.experimental import pallas as pl
from jax.experimental.pallas import tpu as pltpu
from jax.sharding import PartitionSpec as P

AUX_DEV = 128
OCC = 128
MESH = pl.DeviceIdType.MESH
NT = (((1,), (1,)), ((), ()))


def send_half_blocks(nodes, slots, source, vblock, tags, integrals, coeffs, recv, recv_tags,
                     half, send_sem, recv_sem, tag_send, tag_recv, own_sem):
    me = lax.axis_index("aux")
    barrier = pltpu.get_barrier_semaphore()

    @pl.loop(1, nodes)
    def _(k):
        pl.semaphore_signal(
            barrier, inc=1, device_id={"aux": lax.rem(me + k, nodes)}, device_id_type=MESH
        )

    def fill(peer):
        for s in range(slots):
            block = integrals[source[peer, s]]
            panel = coeffs[vblock[peer, s]]
            aux_width, size, inner = block.shape
            out = jnp.dot(
                block.reshape(aux_width * size, inner), panel, preferred_element_type=jnp.float32
            )
            half[peer, s] = out.astype(jnp.bfloat16).reshape(aux_width, size, panel.shape[1])

    half_nodes = nodes // 2
    side, place = me // half_nodes, lax.rem(me, half_nodes)

    def peer_of(i):
        other = lax.rem(side + 1 - i % 2, 2)
        return other * half_nodes + lax.rem(place + i // 2, half_nodes)

    def copies(peer, landed):
        data = pltpu.make_async_remote_copy(
            src_ref=half.at[peer], dst_ref=recv.at[me], send_sem=send_sem.at[peer],
            recv_sem=recv_sem.at[landed], device_id={"aux": peer}, device_id_type=MESH,
        )
        tag = pltpu.make_async_remote_copy(
            src_ref=tags.at[peer], dst_ref=recv_tags.at[me], send_sem=tag_send.at[peer],
            recv_sem=tag_recv.at[landed], device_id={"aux": peer}, device_id_type=MESH,
        )
        return data, tag

    def send(i):
        peer = peer_of(i)
        fill(peer)
        data, tag = copies(peer, me)
        data.start()
        tag.start()

    pl.semaphore_wait(barrier, nodes - 1)
    send(0)
    fill(me)
    own = pltpu.make_async_copy(half.at[me], recv.at[me], own_sem.at[0])
    own_tag = pltpu.make_async_copy(tags.at[me], recv_tags.at[me], own_sem.at[1])
    own.start()
    own_tag.start()

    @pl.loop(2, nodes)
    def _(i):
        send(i)

    own.wait()
    own_tag.wait()

    @pl.loop(1, nodes)
    def _(k):
        peer = lax.rem(me + k, nodes)
        data, tag = copies(peer, peer)
        data.wait()
        tag.wait()


def gram(scale, slots, tags, recv, out, total, fitted, head, following, count, mask):
    nodes, _, aux_width, size, occ = recv.shape
    owned = head.shape[0]
    wide = 2 * size
    groups = out.shape[0] // wide
    out[...] = jnp.zeros_like(out)

    @pl.loop(0, owned)
    def _(a):
        head[a] = 0
        count[a] = 0
        mask[a] = 0

    @pl.loop(0, nodes)
    def _(node):
        for s in range(slots):
            a = tags[node, 2 * s]
            u = tags[node, 2 * s + 1]

            @pl.when(u >= 0)
            def _():
                item = node * slots + s
                following[item] = head[a]
                head[a] = item
                count[a] = count[a] + 1
                mask[a] = mask[a] | (1 << (u // 2))

    @pl.loop(0, owned)
    def _(a):
        bits = mask[a]
        here = [((bits >> i) & 1) == 1 for i in range(groups)]
        spans = [pl.ds(i * wide, wide) for i in range(groups)]

        @pl.when(bits != 0)
        def _():
            for i in range(groups):
                @pl.when(here[i])
                def _():
                    total[spans[i], :] = jnp.zeros((wide, total.shape[1]), jnp.float32)

            def add(_, item):
                node, s = item // slots, item % slots
                u = tags[node, 2 * s + 1]
                rows = pl.ds(pl.multiple_of(u * size, size), size)
                for p in range(aux_width):
                    total[rows, pl.ds(p * occ, occ)] += recv[node, s, p].astype(jnp.float32)
                return following[item]

            lax.fori_loop(0, count[a], add, head[a])
            for i in range(groups):
                @pl.when(here[i])
                def _():
                    fitted[spans[i], :] = total[spans[i], :].astype(jnp.bfloat16)
            for i in range(groups):
                for j in range(groups):
                    @pl.when(here[i] & here[j])
                    def _():
                        out[spans[i], spans[j]] += lax.dot_general(
                            fitted[spans[i], :], fitted[spans[j], :], NT,
                            preferred_element_type=jnp.float32,
                        )

    out[...] = out[...] * scale


def exchange(buf, cols, dims, name, coords, sizes, rank_of, landing, send_sem, recv_sem):
    at = dims.index(name)
    found = []
    for step in range(1, sizes[name]):
        other = lax.rem(coords[name] + step, sizes[name])
        target = dict(coords)
        target[name] = other
        pick = (slice(None),) * at + (other,) + (slice(None),) * (len(dims) - at - 1)
        found.append(
            pltpu.make_async_remote_copy(
                src_ref=buf.at[pick + (slice(None), cols)], dst_ref=landing.at[step - 1],
                send_sem=send_sem.at[step - 1], recv_sem=recv_sem.at[step - 1],
                device_id={"aux": rank_of(target)}, device_id_type=MESH,
            )
        )
    return found


def gathered(buf, cols, dims, name, coords, landing, copies):
    at = dims.index(name)
    pick = (slice(None),) * at + (coords[name],) + (slice(None),) * (len(dims) - at - 1)
    value = buf[pick + (slice(None), cols)]
    for step, copy in enumerate(copies):
        copy.wait()
        value = value + landing[step]
    return value


ORDERS = (("x", "y", "z"), ("y", "z", "x"), ("z", "x", "y"))


def scatter_sum(sizes, part, *refs):
    own, out, first, landed = refs[:4]
    lands = refs[4:13]
    held = refs[13:19]
    send_sem, recv_sem = refs[19:]
    me = lax.axis_index("aux")
    names = ("z", "y", "x", "c")
    coords = {
        "c": me % 2, "x": me // 2 % 2, "y": me // 4 % 2, "z": me // 8,
    }

    def rank_of(c):
        return ((c["z"] * sizes["y"] + c["y"]) * sizes["x"] + c["x"]) * sizes["c"] + c["c"]

    barrier = pltpu.get_barrier_semaphore()
    partners = 0
    for name in names:
        for step in range(1, sizes[name]):
            target = dict(coords)
            target[name] = lax.rem(coords[name] + step, sizes[name])
            pl.semaphore_signal(
                barrier, inc=1, device_id={"aux": rank_of(target)}, device_id_type=MESH
            )
            partners += 1
    pl.semaphore_wait(barrier, partners)

    everything = slice(None)
    copies = exchange(own, everything, names, "c", coords, sizes, rank_of, landed,
                      send_sem.at[9], recv_sem.at[9])
    for copy in copies:
        copy.start()
    first[...] = gathered(own, everything, names, "c", coords, landed, copies)
    bufs = [first] * 3
    left = [list(names[:3]) for _ in range(3)]
    for stage in range(3):
        running = []
        for p in range(3):
            cols = pl.ds(p * part, part) if stage == 0 else slice(None)
            lane = stage * 3 + p
            copies = exchange(bufs[p], cols, left[p], ORDERS[p][stage], coords, sizes, rank_of,
                              lands[lane], send_sem.at[lane], recv_sem.at[lane])
            for copy in copies:
                copy.start()
            running.append((cols, copies))
        for p in range(3):
            cols, copies = running[p]
            value = gathered(bufs[p], cols, left[p], ORDERS[p][stage], coords,
                             lands[stage * 3 + p], copies)
            if stage == 2:
                out[:, pl.ds(p * part, part)] = value
            else:
                bufs[p] = held[stage * 3 + p]
                bufs[p][...] = value
            left[p].remove(ORDERS[p][stage])


def reduce_scatter(matrix, nodes):
    rows, columns = matrix.shape
    sizes = {"z": nodes // 8, "y": 2, "x": 2, "c": 2}
    height, part = rows // nodes, columns // 3
    deepest = max(sizes["z"] - 1, 1)
    lands, held = [], []
    for stage in range(3):
        for p in range(3):
            rest = tuple(sizes[d] for d in ("z", "y", "x") if d not in ORDERS[p][: stage + 1])
            shape = rest + (height, part)
            lands.append(pltpu.VMEM((sizes[ORDERS[p][stage]] - 1,) + shape, jnp.float32))
            if stage < 2:
                held.append(pltpu.VMEM(shape, jnp.float32))
    half = (sizes["z"], 2, 2, height, columns)
    return pl.pallas_call(
        functools.partial(scatter_sum, sizes, part),
        out_shape=jax.ShapeDtypeStruct((height, columns), jnp.float32),
        in_specs=[pl.BlockSpec(memory_space=pltpu.VMEM)],
        out_specs=pl.BlockSpec(memory_space=pltpu.VMEM),
        scratch_shapes=[
            pltpu.VMEM(half, jnp.float32),
            pltpu.VMEM((1,) + half, jnp.float32),
            *lands,
            *held,
            pltpu.SemaphoreType.DMA((10, deepest)),
            pltpu.SemaphoreType.DMA((10, deepest)),
        ],
        compiler_params=pltpu.CompilerParams(
            collective_id=1, has_side_effects=True, vmem_limit_bytes=40 * 2**20
        ),
    )(matrix.reshape(sizes["z"], 2, 2, 2, height, columns))


def fused_body(integrals, block_list, block_count, coeffs):
    stored, aux_width, size, _ = integrals.shape
    basis, occ = coeffs.shape
    nodes = lax.axis_size("aux")
    owned = AUX_DEV // aux_width
    slots = max(2, 64 // nodes)
    positions = jnp.arange(stored, dtype=jnp.int32)
    owner = jnp.where(positions < block_count[0], block_list[:, 0] // owned, nodes)
    before = (owner[:, None] == owner[None, :]) & (positions[None, :] < positions[:, None])
    target = owner * slots + jnp.sum(before.astype(jnp.int32), axis=1)
    chosen = (target[None, :] == jnp.arange(nodes * slots, dtype=jnp.int32)[:, None]).astype(
        jnp.int32
    )
    fields = jnp.stack(
        [positions, block_list[:, 2], block_list[:, 0] % owned, block_list[:, 1] + 1], axis=0
    )
    picked = jnp.sum(chosen[None] * fields[:, None, :], axis=2)
    source = picked[0].reshape(nodes, slots)
    vblock = picked[1].reshape(nodes, slots)
    tags = jnp.stack([picked[2], picked[3] - 1], axis=1).reshape(nodes, 1, 2 * slots)
    tags = jnp.pad(tags, ((0, 0), (0, 0), (0, 128 - 2 * slots)))
    vmem = pl.BlockSpec(memory_space=pltpu.VMEM)
    smem = pl.BlockSpec(memory_space=pltpu.SMEM)
    recv, recv_tags = pl.pallas_call(
        functools.partial(send_half_blocks, nodes, slots),
        out_shape=(
            jax.ShapeDtypeStruct((nodes, slots, aux_width, size, occ), jnp.bfloat16),
            jax.ShapeDtypeStruct((nodes, 1, 128), jnp.int32),
        ),
        in_specs=[smem, smem, vmem, vmem, vmem],
        out_specs=(pl.BlockSpec(memory_space=pl.ANY), vmem),
        scratch_shapes=[
            pltpu.VMEM((nodes, slots, aux_width, size, occ), jnp.bfloat16),
            pltpu.SemaphoreType.DMA((nodes,)),
            pltpu.SemaphoreType.DMA((nodes,)),
            pltpu.SemaphoreType.DMA((nodes,)),
            pltpu.SemaphoreType.DMA((nodes,)),
            pltpu.SemaphoreType.DMA((2,)),
        ],
        compiler_params=pltpu.CompilerParams(
            collective_id=0, has_side_effects=True, vmem_limit_bytes=40 * 2**20
        ),
    )(source, vblock, tags, integrals, coeffs.reshape(basis // size, size, occ))
    matrix = pl.pallas_call(
        functools.partial(gram, 1.0 / (AUX_DEV * nodes * OCC), slots),
        out_shape=jax.ShapeDtypeStruct((basis, basis), jnp.float32),
        in_specs=[smem, vmem],
        out_specs=vmem,
        scratch_shapes=[
            pltpu.VMEM((basis, aux_width * occ), jnp.float32),
            pltpu.VMEM((basis, aux_width * occ), jnp.bfloat16),
            pltpu.SMEM((owned,), jnp.int32),
            pltpu.SMEM((nodes * slots,), jnp.int32),
            pltpu.SMEM((owned,), jnp.int32),
            pltpu.SMEM((owned,), jnp.int32),
        ],
        compiler_params=pltpu.CompilerParams(vmem_limit_bytes=40 * 2**20),
    )(recv_tags.reshape(nodes, 128), recv)
    return reduce_scatter(matrix, nodes)


def body(integrals, block_list, block_count, coeffs):
    stored, aux_width, block_size, _ = integrals.shape
    basis, occ_local = coeffs.shape
    basis_blocks = basis // block_size
    aux_nodes = lax.axis_size("aux")
    owned_blocks = AUX_DEV // aux_width
    slot_count = max(2, 64 // aux_nodes)
    segments = owned_blocks * basis_blocks
    coef_blocks = coeffs.reshape(basis_blocks, block_size, occ_local)
    positions = jnp.arange(stored, dtype=jnp.int32)
    is_live = positions < block_count[0]
    owner_slab = jnp.where(is_live, block_list[:, 0] // owned_blocks, aux_nodes)
    member = (owner_slab[:, None] == jnp.arange(aux_nodes, dtype=jnp.int32)[None, :]).astype(
        jnp.int32
    )
    earlier = jnp.cumsum(member, axis=0) - member
    placed = jnp.sum(earlier * member, axis=1)
    target = jnp.where(is_live, owner_slab * slot_count + placed, aux_nodes * slot_count)
    source = (
        jnp.full((aux_nodes * slot_count + 1,), stored, jnp.int32)
        .at[target]
        .set(positions)[: aux_nodes * slot_count]
    )
    blank_tag = jnp.full((1, 3), -1, jnp.int32)
    send_tags = jnp.concatenate([block_list, blank_tag], axis=0)[source].reshape(
        aux_nodes, slot_count, 3
    )
    recv_tags = lax.all_to_all(send_tags, "aux", split_axis=0, concat_axis=0, tiled=True).reshape(
        aux_nodes * slot_count, 3
    )
    filled = recv_tags[:, 1] >= 0
    seg_of = jnp.where(
        filled, recv_tags[:, 1] * owned_blocks + recv_tags[:, 0] % owned_blocks, segments
    )
    seg_table = (jnp.arange(segments, dtype=jnp.int32)[:, None] == seg_of[None, :]).astype(
        jnp.bfloat16
    )
    padded = jnp.concatenate(
        [integrals, jnp.zeros((1,) + integrals.shape[1:], jnp.bfloat16)], axis=0
    )
    outgoing = padded[source].reshape(aux_nodes, slot_count, aux_width, block_size, block_size)
    lam_index = jnp.where(filled, recv_tags[:, 2], 0)
    recv_coef = coef_blocks[lam_index]
    item_block = lax.all_to_all(outgoing, "aux", split_axis=0, concat_axis=0, tiled=True)
    item_count = item_block.shape[2]
    flat_ints = item_block.reshape(aux_nodes * slot_count, item_count, block_size, block_size)
    half_rows = lax.dot_general(
        flat_ints, recv_coef, (((3,), (1,)), ((0,), (0,))), preferred_element_type=jnp.float32
    ).astype(jnp.bfloat16)
    summed = jnp.dot(
        seg_table, half_rows.reshape(aux_nodes * slot_count, -1), preferred_element_type=jnp.float32
    )
    fitted = summed.reshape(segments, item_count, block_size, occ_local)
    fitted = fitted.astype(jnp.bfloat16).reshape(
        basis_blocks, owned_blocks, aux_width, block_size, occ_local
    )
    fitted = fitted.transpose(0, 3, 1, 2, 4).reshape(basis, owned_blocks * aux_width * occ_local)
    scale_factor = 1.0 / (AUX_DEV * aux_nodes * OCC)
    return lax.psum_scatter(
        lax.dot_general(
            fitted, fitted, (((1,), (1,)), ((), ())), preferred_element_type=jnp.float32
        )
        * scale_factor,
        ("aux", "occ"),
        scatter_dimension=0,
        tiled=True,
    )


def solution(mesh):
    placed = (
        P(("frag", "aux"), None, None, None),
        P(("frag", "aux"), None),
        P(("frag", "aux")),
        P("frag", "occ"),
    )
    simple = mesh.shape["occ"] == 1 and mesh.shape["aux"] % 8 == 0
    return jax.shard_map(
        fused_body if simple else body, mesh=mesh, in_specs=placed, out_specs=P(("frag", "aux", "occ"), None), check_vma=False
    )
```

```python
import functools

import jax
import jax.numpy as jnp
from jax import lax
from jax.experimental import pallas as pl
from jax.experimental.pallas import tpu as pltpu
from jax.sharding import PartitionSpec as P

AUX_DEV = 128
OCC = 128
MESH = pl.DeviceIdType.MESH
NT = (((1,), (1,)), ((), ()))


def send_half_blocks(nodes, slots, source, vblock, tags, integrals, coeffs, recv, recv_tags,
                     half, send_sem, recv_sem, tag_send, tag_recv, own_sem):
    me = lax.axis_index("aux")
    barrier = pltpu.get_barrier_semaphore()

    @pl.loop(1, nodes)
    def _(k):
        pl.semaphore_signal(
            barrier, inc=1, device_id={"aux": lax.rem(me + k, nodes)}, device_id_type=MESH
        )

    def fill(peer):
        for s in range(slots):
            block = integrals[source[peer, s]]
            panel = coeffs[vblock[peer, s]]
            aux_width, size, inner = block.shape
            out = jnp.dot(
                block.reshape(aux_width * size, inner), panel, preferred_element_type=jnp.float32
            )
            half[peer, s] = out.astype(jnp.bfloat16).reshape(aux_width, size, panel.shape[1])

    def peer_of(i):
        pair = i // 2
        flips = (1 - i % 2) * (nodes // 2) + pair % 2 * (nodes // 4) + pair // 2
        peer, bit = 0, 1
        while bit < nodes:
            peer = peer + (me // bit + flips // bit) % 2 * bit
            bit *= 2
        return peer

    def copies(peer, landed):
        data = pltpu.make_async_remote_copy(
            src_ref=half.at[peer], dst_ref=recv.at[me], send_sem=send_sem.at[peer],
            recv_sem=recv_sem.at[landed], device_id={"aux": peer}, device_id_type=MESH,
        )
        tag = pltpu.make_async_remote_copy(
            src_ref=tags.at[peer], dst_ref=recv_tags.at[me], send_sem=tag_send.at[peer],
            recv_sem=tag_recv.at[landed], device_id={"aux": peer}, device_id_type=MESH,
        )
        return data, tag

    def send(i):
        peer = peer_of(i)
        fill(peer)
        data, tag = copies(peer, me)
        data.start()
        tag.start()

    pl.semaphore_wait(barrier, nodes - 1)
    send(0)
    fill(me)
    own = pltpu.make_async_copy(half.at[me], recv.at[me], own_sem.at[0])
    own_tag = pltpu.make_async_copy(tags.at[me], recv_tags.at[me], own_sem.at[1])
    own.start()
    own_tag.start()

    @pl.loop(2, nodes)
    def _(i):
        send(i)

    own.wait()
    own_tag.wait()

    @pl.loop(1, nodes)
    def _(k):
        peer = lax.rem(me + k, nodes)
        data, tag = copies(peer, peer)
        data.wait()
        tag.wait()


def gram(scale, slots, tags, recv, out, total, fitted, head, following, count, mask):
    nodes, _, aux_width, size, occ = recv.shape
    owned = head.shape[0]
    wide = 2 * size
    groups = out.shape[0] // wide
    out[...] = jnp.zeros_like(out)

    @pl.loop(0, owned)
    def _(a):
        head[a] = 0
        count[a] = 0
        mask[a] = 0

    @pl.loop(0, nodes * slots)
    def _(item):
        following[item] = 0

    @pl.loop(0, nodes)
    def _(node):
        for s in range(slots):
            a = tags[node, 2 * s]
            u = tags[node, 2 * s + 1]

            @pl.when(u >= 0)
            def _():
                item = node * slots + s
                following[item] = head[a]
                head[a] = item
                count[a] = count[a] + 1
                mask[a] = mask[a] | (1 << (u // 2))

    @pl.loop(0, owned)
    def _(a):
        bits = mask[a]
        here = [((bits >> i) & 1) == 1 for i in range(groups)]
        spans = [pl.ds(i * wide, wide) for i in range(groups)]

        members = count[a]
        item = head[a]
        second = following[item]
        row = tags[item // slots, 2 * (item % slots) + 1]
        row_second = tags[second // slots, 2 * (second % slots) + 1]
        two = (members == 2) & (row != row_second)

        def panel(which):
            node, s = which // slots, which % slots
            return jnp.concatenate([recv[node, s, p] for p in range(aux_width)], axis=1)

        def span(u):
            return pl.ds(pl.multiple_of(u * size, size), size)

        @pl.when(members == 1)
        def _():
            x = panel(item)
            out[span(row), span(row)] += lax.dot_general(
                x, x, NT, preferred_element_type=jnp.float32
            )

        @pl.when(two)
        def _():
            x = jnp.concatenate([panel(item), panel(second)], axis=0)
            product = lax.dot_general(x, x, NT, preferred_element_type=jnp.float32)
            out[span(row), span(row)] += product[:size, :size]
            out[span(row), span(row_second)] += product[:size, size:]
            out[span(row_second), span(row)] += product[size:, :size]
            out[span(row_second), span(row_second)] += product[size:, size:]

        @pl.when((members > 1) & jnp.logical_not(two))
        def _():
            for i in range(groups):
                @pl.when(here[i])
                def _():
                    total[spans[i], :] = jnp.zeros((wide, total.shape[1]), jnp.float32)

            def add(_, item):
                node, s = item // slots, item % slots
                u = tags[node, 2 * s + 1]
                rows = pl.ds(pl.multiple_of(u * size, size), size)
                for p in range(aux_width):
                    total[rows, pl.ds(p * occ, occ)] += recv[node, s, p].astype(jnp.float32)
                return following[item]

            lax.fori_loop(0, count[a], add, head[a])
            for i in range(groups):
                @pl.when(here[i])
                def _():
                    fitted[spans[i], :] = total[spans[i], :].astype(jnp.bfloat16)
            for i in range(groups):
                for j in range(groups):
                    @pl.when(here[i] & here[j])
                    def _():
                        out[spans[i], spans[j]] += lax.dot_general(
                            fitted[spans[i], :], fitted[spans[j], :], NT,
                            preferred_element_type=jnp.float32,
                        )

    out[...] = out[...] * scale


def exchange(buf, cols, dims, name, coords, sizes, rank_of, landing, send_sem, recv_sem):
    at = dims.index(name)
    found = []
    for step in range(1, sizes[name]):
        other = lax.rem(coords[name] + step, sizes[name])
        target = dict(coords)
        target[name] = other
        pick = (slice(None),) * at + (other,) + (slice(None),) * (len(dims) - at - 1)
        found.append(
            pltpu.make_async_remote_copy(
                src_ref=buf.at[pick + (slice(None), cols)], dst_ref=landing.at[step - 1],
                send_sem=send_sem.at[step - 1], recv_sem=recv_sem.at[step - 1],
                device_id={"aux": rank_of(target)}, device_id_type=MESH,
            )
        )
    return found


def gathered(buf, cols, dims, name, coords, landing, copies):
    at = dims.index(name)
    pick = (slice(None),) * at + (coords[name],) + (slice(None),) * (len(dims) - at - 1)
    value = buf[pick + (slice(None), cols)]
    for step, copy in enumerate(copies):
        copy.wait()
        value = value + landing[step]
    return value


ORDERS = (("x", "y", "z"), ("y", "z", "x"), ("z", "x", "y"))


def scatter_sum(sizes, starts, *refs):
    own, out = refs[:2]
    lands = refs[2:14]
    held = refs[14:23]
    send_sem, recv_sem = refs[23:]
    me = lax.axis_index("aux")
    names = ("z", "y", "x", "c")
    coords = {
        "c": me % 2, "x": me // 2 % 2, "y": me // 4 % 2, "z": me // 8,
    }

    def rank_of(c):
        return ((c["z"] * sizes["y"] + c["y"]) * sizes["x"] + c["x"]) * sizes["c"] + c["c"]

    barrier = pltpu.get_barrier_semaphore()
    partners = 0
    for name in names:
        for step in range(1, sizes[name]):
            target = dict(coords)
            target[name] = lax.rem(coords[name] + step, sizes[name])
            pl.semaphore_signal(
                barrier, inc=1, device_id={"aux": rank_of(target)}, device_id_type=MESH
            )
            partners += 1
    pl.semaphore_wait(barrier, partners)

    orders = [("c",) + order for order in ORDERS]
    bufs = [own] * 3
    left = [list(names) for _ in range(3)]
    spans = [pl.ds(starts[p], starts[p + 1] - starts[p]) for p in range(3)]

    def start(p, stage):
        cols = spans[p] if stage == 0 else slice(None)
        lane = stage * 3 + p
        copies = exchange(bufs[p], cols, left[p], orders[p][stage], coords, sizes, rank_of,
                          lands[lane], send_sem.at[lane], recv_sem.at[lane])
        for copy in copies:
            copy.start()
        return cols, copies

    running = [start(p, 0) for p in range(3)]
    for stage in range(4):
        for p in range(3):
            cols, copies = running[p]
            value = gathered(bufs[p], cols, left[p], orders[p][stage], coords,
                             lands[stage * 3 + p], copies)
            if stage == 3:
                out[:, spans[p]] = value
                continue
            bufs[p] = held[stage * 3 + p]
            bufs[p][...] = value
            left[p].remove(orders[p][stage])
            running[p] = start(p, stage + 1)


def reduce_scatter(matrix, nodes):
    rows, columns = matrix.shape
    sizes = {"z": nodes // 8, "y": 2, "x": 2, "c": 2}
    height = rows // nodes
    starts = (0, columns // 2, columns // 6 * 5, columns)
    deepest = max(sizes["z"] - 1, 1)
    lands, held = [], []
    for stage in range(4):
        for p in range(3):
            done = ("c",) + ORDERS[p][:stage]
            rest = tuple(sizes[d] for d in ("z", "y", "x") if d not in done)
            shape = rest + (height, starts[p + 1] - starts[p])
            axis = done[-1]
            lands.append(pltpu.VMEM((sizes[axis] - 1,) + shape, jnp.float32))
            if stage < 3:
                held.append(pltpu.VMEM(shape, jnp.float32))
    return pl.pallas_call(
        functools.partial(scatter_sum, sizes, starts),
        out_shape=jax.ShapeDtypeStruct((height, columns), jnp.float32),
        in_specs=[pl.BlockSpec(memory_space=pltpu.VMEM)],
        out_specs=pl.BlockSpec(memory_space=pltpu.VMEM),
        scratch_shapes=[
            *lands,
            *held,
            pltpu.SemaphoreType.DMA((12, deepest)),
            pltpu.SemaphoreType.DMA((12, deepest)),
        ],
        compiler_params=pltpu.CompilerParams(
            collective_id=1, has_side_effects=True, vmem_limit_bytes=40 * 2**20
        ),
    )(matrix.reshape(sizes["z"], 2, 2, 2, height, columns))


def fused_body(integrals, block_list, block_count, coeffs):
    stored, aux_width, size, _ = integrals.shape
    basis, occ = coeffs.shape
    nodes = lax.axis_size("aux")
    owned = AUX_DEV // aux_width
    slots = max(2, 64 // nodes)
    positions = jnp.arange(stored, dtype=jnp.int32)
    owner = jnp.where(positions < block_count[0], block_list[:, 0] // owned, nodes)
    before = (owner[:, None] == owner[None, :]) & (positions[None, :] < positions[:, None])
    target = owner * slots + jnp.sum(before.astype(jnp.int32), axis=1)
    chosen = (target[None, :] == jnp.arange(nodes * slots, dtype=jnp.int32)[:, None]).astype(
        jnp.int32
    )
    fields = jnp.stack(
        [positions, block_list[:, 2], block_list[:, 0] % owned, block_list[:, 1] + 1], axis=0
    )
    picked = jnp.sum(chosen[None] * fields[:, None, :], axis=2)
    source = picked[0].reshape(nodes, slots)
    vblock = picked[1].reshape(nodes, slots)
    tags = jnp.stack([picked[2], picked[3] - 1], axis=1).reshape(nodes, 1, 2 * slots)
    tags = jnp.pad(tags, ((0, 0), (0, 0), (0, 128 - 2 * slots)))
    vmem = pl.BlockSpec(memory_space=pltpu.VMEM)
    smem = pl.BlockSpec(memory_space=pltpu.SMEM)
    recv, recv_tags = pl.pallas_call(
        functools.partial(send_half_blocks, nodes, slots),
        out_shape=(
            jax.ShapeDtypeStruct((nodes, slots, aux_width, size, occ), jnp.bfloat16),
            jax.ShapeDtypeStruct((nodes, 1, 128), jnp.int32),
        ),
        in_specs=[smem, smem, vmem, vmem, vmem],
        out_specs=(pl.BlockSpec(memory_space=pl.ANY), vmem),
        scratch_shapes=[
            pltpu.VMEM((nodes, slots, aux_width, size, occ), jnp.bfloat16),
            pltpu.SemaphoreType.DMA((nodes,)),
            pltpu.SemaphoreType.DMA((nodes,)),
            pltpu.SemaphoreType.DMA((nodes,)),
            pltpu.SemaphoreType.DMA((nodes,)),
            pltpu.SemaphoreType.DMA((2,)),
        ],
        compiler_params=pltpu.CompilerParams(
            collective_id=0, has_side_effects=True, vmem_limit_bytes=40 * 2**20
        ),
    )(source, vblock, tags, integrals, coeffs.reshape(basis // size, size, occ))
    matrix = pl.pallas_call(
        functools.partial(gram, 1.0 / (AUX_DEV * nodes * OCC), slots),
        out_shape=jax.ShapeDtypeStruct((basis, basis), jnp.float32),
        in_specs=[smem, vmem],
        out_specs=vmem,
        scratch_shapes=[
            pltpu.VMEM((basis, aux_width * occ), jnp.float32),
            pltpu.VMEM((basis, aux_width * occ), jnp.bfloat16),
            pltpu.SMEM((owned,), jnp.int32),
            pltpu.SMEM((nodes * slots,), jnp.int32),
            pltpu.SMEM((owned,), jnp.int32),
            pltpu.SMEM((owned,), jnp.int32),
        ],
        compiler_params=pltpu.CompilerParams(vmem_limit_bytes=40 * 2**20),
    )(recv_tags.reshape(nodes, 128), recv)
    return reduce_scatter(matrix, nodes)


def body(integrals, block_list, block_count, coeffs):
    stored, aux_width, block_size, _ = integrals.shape
    basis, occ_local = coeffs.shape
    basis_blocks = basis // block_size
    aux_nodes = lax.axis_size("aux")
    owned_blocks = AUX_DEV // aux_width
    slot_count = max(2, 64 // aux_nodes)
    segments = owned_blocks * basis_blocks
    coef_blocks = coeffs.reshape(basis_blocks, block_size, occ_local)
    positions = jnp.arange(stored, dtype=jnp.int32)
    is_live = positions < block_count[0]
    owner_slab = jnp.where(is_live, block_list[:, 0] // owned_blocks, aux_nodes)
    member = (owner_slab[:, None] == jnp.arange(aux_nodes, dtype=jnp.int32)[None, :]).astype(
        jnp.int32
    )
    earlier = jnp.cumsum(member, axis=0) - member
    placed = jnp.sum(earlier * member, axis=1)
    target = jnp.where(is_live, owner_slab * slot_count + placed, aux_nodes * slot_count)
    source = (
        jnp.full((aux_nodes * slot_count + 1,), stored, jnp.int32)
        .at[target]
        .set(positions)[: aux_nodes * slot_count]
    )
    blank_tag = jnp.full((1, 3), -1, jnp.int32)
    send_tags = jnp.concatenate([block_list, blank_tag], axis=0)[source].reshape(
        aux_nodes, slot_count, 3
    )
    recv_tags = lax.all_to_all(send_tags, "aux", split_axis=0, concat_axis=0, tiled=True).reshape(
        aux_nodes * slot_count, 3
    )
    filled = recv_tags[:, 1] >= 0
    seg_of = jnp.where(
        filled, recv_tags[:, 1] * owned_blocks + recv_tags[:, 0] % owned_blocks, segments
    )
    seg_table = (jnp.arange(segments, dtype=jnp.int32)[:, None] == seg_of[None, :]).astype(
        jnp.bfloat16
    )
    padded = jnp.concatenate(
        [integrals, jnp.zeros((1,) + integrals.shape[1:], jnp.bfloat16)], axis=0
    )
    outgoing = padded[source].reshape(aux_nodes, slot_count, aux_width, block_size, block_size)
    lam_index = jnp.where(filled, recv_tags[:, 2], 0)
    recv_coef = coef_blocks[lam_index]
    item_block = lax.all_to_all(outgoing, "aux", split_axis=0, concat_axis=0, tiled=True)
    item_count = item_block.shape[2]
    flat_ints = item_block.reshape(aux_nodes * slot_count, item_count, block_size, block_size)
    half_rows = lax.dot_general(
        flat_ints, recv_coef, (((3,), (1,)), ((0,), (0,))), preferred_element_type=jnp.float32
    ).astype(jnp.bfloat16)
    summed = jnp.dot(
        seg_table, half_rows.reshape(aux_nodes * slot_count, -1), preferred_element_type=jnp.float32
    )
    fitted = summed.reshape(segments, item_count, block_size, occ_local)
    fitted = fitted.astype(jnp.bfloat16).reshape(
        basis_blocks, owned_blocks, aux_width, block_size, occ_local
    )
    fitted = fitted.transpose(0, 3, 1, 2, 4).reshape(basis, owned_blocks * aux_width * occ_local)
    scale_factor = 1.0 / (AUX_DEV * aux_nodes * OCC)
    return lax.psum_scatter(
        lax.dot_general(
            fitted, fitted, (((1,), (1,)), ((), ())), preferred_element_type=jnp.float32
        )
        * scale_factor,
        ("aux", "occ"),
        scatter_dimension=0,
        tiled=True,
    )


def solution(mesh):
    placed = (
        P(("frag", "aux"), None, None, None),
        P(("frag", "aux"), None),
        P(("frag", "aux")),
        P("frag", "occ"),
    )
    simple = mesh.shape["occ"] == 1 and mesh.shape["aux"] in (8, 16, 32, 64)
    return jax.shard_map(
        fused_body if simple else body, mesh=mesh, in_specs=placed, out_specs=P(("frag", "aux", "occ"), None), check_vma=False
    )
```

```python
import functools

import jax
import jax.numpy as jnp
from jax import lax
from jax.experimental import pallas as pl
from jax.experimental.pallas import tpu as pltpu
from jax.sharding import PartitionSpec as P

AUX_DEV = 128
OCC = 128
MESH = pl.DeviceIdType.MESH
NT = (((1,), (1,)), ((), ()))


def send_half_blocks(nodes, slots, source, vblock, tags, integrals, coeffs, recv, recv_tags,
                     half, send_sem, recv_sem, tag_send, tag_recv, own_sem):
    me = lax.axis_index("aux")
    barrier = pltpu.get_barrier_semaphore()

    @pl.loop(1, nodes)
    def _(k):
        pl.semaphore_signal(
            barrier, inc=1, device_id={"aux": lax.rem(me + k, nodes)}, device_id_type=MESH
        )

    def fill(peer):
        for s in range(slots):
            block = integrals[source[peer, s]]
            panel = coeffs[vblock[peer, s]]
            aux_width, size, inner = block.shape
            out = jnp.dot(
                block.reshape(aux_width * size, inner), panel, preferred_element_type=jnp.float32
            )
            half[peer, s] = out.astype(jnp.bfloat16).reshape(aux_width, size, panel.shape[1])

    def peer_of(i):
        pair = i // 2
        flips = (1 - i % 2) * (nodes // 2) + pair % 2 * (nodes // 4) + pair // 2
        peer, bit = 0, 1
        while bit < nodes:
            peer = peer + (me // bit + flips // bit) % 2 * bit
            bit *= 2
        return peer

    def copies(peer, landed):
        data = pltpu.make_async_remote_copy(
            src_ref=half.at[peer], dst_ref=recv.at[me], send_sem=send_sem.at[peer],
            recv_sem=recv_sem.at[landed], device_id={"aux": peer}, device_id_type=MESH,
        )
        tag = pltpu.make_async_remote_copy(
            src_ref=tags.at[peer], dst_ref=recv_tags.at[me], send_sem=tag_send.at[peer],
            recv_sem=tag_recv.at[landed], device_id={"aux": peer}, device_id_type=MESH,
        )
        return data, tag

    def send(i):
        peer = peer_of(i)
        fill(peer)
        data, tag = copies(peer, me)
        data.start()
        tag.start()

    pl.semaphore_wait(barrier, nodes - 1)
    send(0)
    fill(me)
    own = pltpu.make_async_copy(half.at[me], recv.at[me], own_sem.at[0])
    own_tag = pltpu.make_async_copy(tags.at[me], recv_tags.at[me], own_sem.at[1])
    own.start()
    own_tag.start()

    @pl.loop(2, nodes)
    def _(i):
        send(i)

    own.wait()
    own_tag.wait()

    @pl.loop(1, nodes)
    def _(k):
        peer = lax.rem(me + k, nodes)
        data, tag = copies(peer, peer)
        data.wait()
        tag.wait()


def gram(scale, slots, tags, recv, out, total, fitted, head, following, count, distinct, rows):
    nodes, _, aux_width, size, occ = recv.shape
    groups = out.shape[0] // size
    owned = distinct.shape[0]
    out[...] = jnp.zeros_like(out)

    @pl.loop(0, owned)
    def _(a):
        distinct[a] = 0
        for u in range(groups):
            count[a * groups + u] = 0
            head[a * groups + u] = 0
            rows[a * groups + u] = 0

    @pl.loop(0, nodes)
    def _(node):
        for s in range(slots):
            a = tags[node, 2 * s]
            u = tags[node, 2 * s + 1]

            @pl.when(u >= 0)
            def _():
                item = node * slots + s
                segment = a * groups + u
                seen = count[segment]

                @pl.when(seen == 0)
                def _():
                    rows[a * groups + distinct[a]] = u
                    distinct[a] = distinct[a] + 1

                following[item] = head[segment]
                head[segment] = item
                count[segment] = seen + 1

    def panel(which):
        node, s = which // slots, which % slots
        return jnp.concatenate([recv[node, s, p] for p in range(aux_width)], axis=1)

    def span(u):
        return pl.ds(pl.multiple_of(u * size, size), size)

    @pl.loop(0, owned)
    def _(a):
        present = distinct[a]
        base = a * groups
        first, second = rows[base], rows[base + 1]
        once = (count[base + first] == 1) & ((present < 2) | (count[base + second] == 1))
        simple = once & (present < 3)

        @pl.when(simple & (present == 1))
        def _():
            x = panel(head[base + first])
            out[span(first), span(first)] += lax.dot_general(
                x, x, NT, preferred_element_type=jnp.float32
            )

        @pl.when(simple & (present == 2))
        def _():
            x = jnp.concatenate(
                [panel(head[base + first]), panel(head[base + second])], axis=0
            )
            product = lax.dot_general(x, x, NT, preferred_element_type=jnp.float32)
            out[span(first), span(first)] += product[:size, :size]
            out[span(first), span(second)] += product[:size, size:]
            out[span(second), span(first)] += product[size:, :size]
            out[span(second), span(second)] += product[size:, size:]

        @pl.when((present > 0) & jnp.logical_not(simple))
        def _():
            @pl.loop(0, present)
            def _(i):
                segment = base + rows[base + i]
                item = head[segment]
                members = count[segment]

                @pl.when(members == 1)
                def _():
                    fitted[span(i), :] = panel(item)

                @pl.when(members > 1)
                def _():
                    total[...] = panel(item).astype(jnp.float32)

                    def add(_, item):
                        total[...] += panel(item).astype(jnp.float32)
                        return following[item]

                    lax.fori_loop(1, members, add, following[item])
                    fitted[span(i), :] = total[...].astype(jnp.bfloat16)

            for k in range(1, groups + 1):
                @pl.when(present == k)
                def _():
                    for low in range(0, k, 2):
                        high = min(low + 2, k)
                        product = lax.dot_general(
                            fitted[low * size : high * size, :], fitted[: k * size, :], NT,
                            preferred_element_type=jnp.float32,
                        )
                        for i in range(low, high):
                            for j in range(k):
                                out[span(rows[base + i]), span(rows[base + j])] += product[
                                    (i - low) * size : (i - low + 1) * size,
                                    j * size : (j + 1) * size,
                                ]

    out[...] = out[...] * scale


def exchange(buf, cols, dims, name, coords, sizes, rank_of, landing, send_sem, recv_sem):
    at = dims.index(name)
    found = []
    for step in range(1, sizes[name]):
        other = lax.rem(coords[name] + step, sizes[name])
        target = dict(coords)
        target[name] = other
        pick = (slice(None),) * at + (other,) + (slice(None),) * (len(dims) - at - 1)
        found.append(
            pltpu.make_async_remote_copy(
                src_ref=buf.at[pick + (slice(None), cols)], dst_ref=landing.at[step - 1],
                send_sem=send_sem.at[step - 1], recv_sem=recv_sem.at[step - 1],
                device_id={"aux": rank_of(target)}, device_id_type=MESH,
            )
        )
    return found


def gathered(buf, cols, dims, name, coords, landing, copies):
    at = dims.index(name)
    pick = (slice(None),) * at + (coords[name],) + (slice(None),) * (len(dims) - at - 1)
    value = buf[pick + (slice(None), cols)]
    for step, copy in enumerate(copies):
        copy.wait()
        value = value + landing[step]
    return value


ORDERS = (("x", "y", "z"), ("y", "z", "x"), ("z", "x", "y"))


def scatter_sum(sizes, starts, *refs):
    own, out = refs[:2]
    lands = refs[2:14]
    held = refs[14:23]
    send_sem, recv_sem = refs[23:]
    me = lax.axis_index("aux")
    names = ("z", "y", "x", "c")
    coords = {
        "c": me % 2, "x": me // 2 % 2, "y": me // 4 % 2, "z": me // 8,
    }

    def rank_of(c):
        return ((c["z"] * sizes["y"] + c["y"]) * sizes["x"] + c["x"]) * sizes["c"] + c["c"]

    barrier = pltpu.get_barrier_semaphore()
    partners = 0
    for name in names:
        for step in range(1, sizes[name]):
            target = dict(coords)
            target[name] = lax.rem(coords[name] + step, sizes[name])
            pl.semaphore_signal(
                barrier, inc=1, device_id={"aux": rank_of(target)}, device_id_type=MESH
            )
            partners += 1
    pl.semaphore_wait(barrier, partners)

    orders = [("c",) + order for order in ORDERS]
    bufs = [own] * 3
    left = [list(names) for _ in range(3)]
    spans = [pl.ds(starts[p], starts[p + 1] - starts[p]) for p in range(3)]

    def start(p, stage):
        cols = spans[p] if stage == 0 else slice(None)
        lane = stage * 3 + p
        copies = exchange(bufs[p], cols, left[p], orders[p][stage], coords, sizes, rank_of,
                          lands[lane], send_sem.at[lane], recv_sem.at[lane])
        for copy in copies:
            copy.start()
        return cols, copies

    running = [start(p, 0) for p in range(3)]
    for stage in range(4):
        for p in range(3):
            cols, copies = running[p]
            value = gathered(bufs[p], cols, left[p], orders[p][stage], coords,
                             lands[stage * 3 + p], copies)
            if stage == 3:
                out[:, spans[p]] = value
                continue
            bufs[p] = held[stage * 3 + p]
            bufs[p][...] = value
            left[p].remove(orders[p][stage])
            running[p] = start(p, stage + 1)


def reduce_scatter(matrix, nodes):
    rows, columns = matrix.shape
    sizes = {"z": nodes // 8, "y": 2, "x": 2, "c": 2}
    height = rows // nodes
    starts = (0, columns // 2, columns // 6 * 5, columns)
    deepest = max(sizes["z"] - 1, 1)
    lands, held = [], []
    for stage in range(4):
        for p in range(3):
            done = ("c",) + ORDERS[p][:stage]
            rest = tuple(sizes[d] for d in ("z", "y", "x") if d not in done)
            shape = rest + (height, starts[p + 1] - starts[p])
            axis = done[-1]
            lands.append(pltpu.VMEM((sizes[axis] - 1,) + shape, jnp.float32))
            if stage < 3:
                held.append(pltpu.VMEM(shape, jnp.float32))
    return pl.pallas_call(
        functools.partial(scatter_sum, sizes, starts),
        out_shape=jax.ShapeDtypeStruct((height, columns), jnp.float32),
        in_specs=[pl.BlockSpec(memory_space=pltpu.VMEM)],
        out_specs=pl.BlockSpec(memory_space=pltpu.VMEM),
        scratch_shapes=[
            *lands,
            *held,
            pltpu.SemaphoreType.DMA((12, deepest)),
            pltpu.SemaphoreType.DMA((12, deepest)),
        ],
        compiler_params=pltpu.CompilerParams(
            collective_id=1, has_side_effects=True, vmem_limit_bytes=40 * 2**20
        ),
    )(matrix.reshape(sizes["z"], 2, 2, 2, height, columns))


def fused_body(integrals, block_list, block_count, coeffs):
    stored, aux_width, size, _ = integrals.shape
    basis, occ = coeffs.shape
    nodes = lax.axis_size("aux")
    owned = AUX_DEV // aux_width
    slots = max(2, 64 // nodes)
    positions = jnp.arange(stored, dtype=jnp.int32)
    slab = lax.div(block_list[:, 0], jnp.int32(owned))
    owner = jnp.where(positions < block_count[0], slab, nodes)
    before = (owner[:, None] == owner[None, :]) & (positions[None, :] < positions[:, None])
    target = owner * slots + jnp.sum(before.astype(jnp.int32), axis=1)
    chosen = (target[None, :] == jnp.arange(nodes * slots, dtype=jnp.int32)[:, None]).astype(
        jnp.int32
    )
    fields = jnp.stack(
        [positions, block_list[:, 2], block_list[:, 0] - slab * owned, block_list[:, 1] + 1], axis=0
    )
    picked = jnp.sum(chosen[None] * fields[:, None, :], axis=2)
    source = picked[0].reshape(nodes, slots)
    vblock = picked[1].reshape(nodes, slots)
    tags = jnp.stack([picked[2], picked[3] - 1], axis=1).reshape(nodes, 1, 2 * slots)
    tags = jnp.pad(tags, ((0, 0), (0, 0), (0, 128 - 2 * slots)))
    vmem = pl.BlockSpec(memory_space=pltpu.VMEM)
    smem = pl.BlockSpec(memory_space=pltpu.SMEM)
    recv, recv_tags = pl.pallas_call(
        functools.partial(send_half_blocks, nodes, slots),
        out_shape=(
            jax.ShapeDtypeStruct((nodes, slots, aux_width, size, occ), jnp.bfloat16),
            jax.ShapeDtypeStruct((nodes, 1, 128), jnp.int32),
        ),
        in_specs=[smem, smem, vmem, vmem, vmem],
        out_specs=(pl.BlockSpec(memory_space=pl.ANY), vmem),
        scratch_shapes=[
            pltpu.VMEM((nodes, slots, aux_width, size, occ), jnp.bfloat16),
            pltpu.SemaphoreType.DMA((nodes,)),
            pltpu.SemaphoreType.DMA((nodes,)),
            pltpu.SemaphoreType.DMA((nodes,)),
            pltpu.SemaphoreType.DMA((nodes,)),
            pltpu.SemaphoreType.DMA((2,)),
        ],
        compiler_params=pltpu.CompilerParams(
            collective_id=0, has_side_effects=True, vmem_limit_bytes=40 * 2**20
        ),
    )(source, vblock, tags, integrals, coeffs.reshape(basis // size, size, occ))
    matrix = pl.pallas_call(
        functools.partial(gram, 1.0 / (AUX_DEV * nodes * OCC), slots),
        out_shape=jax.ShapeDtypeStruct((basis, basis), jnp.float32),
        in_specs=[smem, vmem],
        out_specs=vmem,
        scratch_shapes=[
            pltpu.VMEM((size, aux_width * occ), jnp.float32),
            pltpu.VMEM((basis, aux_width * occ), jnp.bfloat16),
            pltpu.SMEM((owned * (basis // size),), jnp.int32),
            pltpu.SMEM((nodes * slots,), jnp.int32),
            pltpu.SMEM((owned * (basis // size),), jnp.int32),
            pltpu.SMEM((owned,), jnp.int32),
            pltpu.SMEM((owned * (basis // size),), jnp.int32),
        ],
        compiler_params=pltpu.CompilerParams(vmem_limit_bytes=40 * 2**20),
    )(recv_tags.reshape(nodes, 128), recv)
    return reduce_scatter(matrix, nodes)


def body(integrals, block_list, block_count, coeffs):
    stored, aux_width, block_size, _ = integrals.shape
    basis, occ_local = coeffs.shape
    basis_blocks = basis // block_size
    aux_nodes = lax.axis_size("aux")
    owned_blocks = AUX_DEV // aux_width
    slot_count = max(2, 64 // aux_nodes)
    segments = owned_blocks * basis_blocks
    coef_blocks = coeffs.reshape(basis_blocks, block_size, occ_local)
    positions = jnp.arange(stored, dtype=jnp.int32)
    is_live = positions < block_count[0]
    owner_slab = jnp.where(is_live, block_list[:, 0] // owned_blocks, aux_nodes)
    member = (owner_slab[:, None] == jnp.arange(aux_nodes, dtype=jnp.int32)[None, :]).astype(
        jnp.int32
    )
    earlier = jnp.cumsum(member, axis=0) - member
    placed = jnp.sum(earlier * member, axis=1)
    target = jnp.where(is_live, owner_slab * slot_count + placed, aux_nodes * slot_count)
    source = (
        jnp.full((aux_nodes * slot_count + 1,), stored, jnp.int32)
        .at[target]
        .set(positions)[: aux_nodes * slot_count]
    )
    blank_tag = jnp.full((1, 3), -1, jnp.int32)
    send_tags = jnp.concatenate([block_list, blank_tag], axis=0)[source].reshape(
        aux_nodes, slot_count, 3
    )
    recv_tags = lax.all_to_all(send_tags, "aux", split_axis=0, concat_axis=0, tiled=True).reshape(
        aux_nodes * slot_count, 3
    )
    filled = recv_tags[:, 1] >= 0
    seg_of = jnp.where(
        filled, recv_tags[:, 1] * owned_blocks + recv_tags[:, 0] % owned_blocks, segments
    )
    seg_table = (jnp.arange(segments, dtype=jnp.int32)[:, None] == seg_of[None, :]).astype(
        jnp.bfloat16
    )
    padded = jnp.concatenate(
        [integrals, jnp.zeros((1,) + integrals.shape[1:], jnp.bfloat16)], axis=0
    )
    outgoing = padded[source].reshape(aux_nodes, slot_count, aux_width, block_size, block_size)
    lam_index = jnp.where(filled, recv_tags[:, 2], 0)
    recv_coef = coef_blocks[lam_index]
    item_block = lax.all_to_all(outgoing, "aux", split_axis=0, concat_axis=0, tiled=True)
    item_count = item_block.shape[2]
    flat_ints = item_block.reshape(aux_nodes * slot_count, item_count, block_size, block_size)
    half_rows = lax.dot_general(
        flat_ints, recv_coef, (((3,), (1,)), ((0,), (0,))), preferred_element_type=jnp.float32
    ).astype(jnp.bfloat16)
    summed = jnp.dot(
        seg_table, half_rows.reshape(aux_nodes * slot_count, -1), preferred_element_type=jnp.float32
    )
    fitted = summed.reshape(segments, item_count, block_size, occ_local)
    fitted = fitted.astype(jnp.bfloat16).reshape(
        basis_blocks, owned_blocks, aux_width, block_size, occ_local
    )
    fitted = fitted.transpose(0, 3, 1, 2, 4).reshape(basis, owned_blocks * aux_width * occ_local)
    scale_factor = 1.0 / (AUX_DEV * aux_nodes * OCC)
    return lax.psum_scatter(
        lax.dot_general(
            fitted, fitted, (((1,), (1,)), ((), ())), preferred_element_type=jnp.float32
        )
        * scale_factor,
        ("aux", "occ"),
        scatter_dimension=0,
        tiled=True,
    )


def solution(mesh):
    placed = (
        P(("frag", "aux"), None, None, None),
        P(("frag", "aux"), None),
        P(("frag", "aux")),
        P("frag", "occ"),
    )
    simple = mesh.shape["occ"] == 1 and mesh.shape["aux"] in (8, 16, 32, 64)
    return jax.shard_map(
        fused_body if simple else body, mesh=mesh, in_specs=placed, out_specs=P(("frag", "aux", "occ"), None), check_vma=False
    )
```

```python
import functools

import jax
import jax.numpy as jnp
from jax import lax
from jax.experimental import pallas as pl
from jax.experimental.pallas import tpu as pltpu
from jax.sharding import PartitionSpec as P

AUX_DEV = 128
OCC = 128
MESH = pl.DeviceIdType.MESH
NT = (((1,), (1,)), ((), ()))


def send_half_blocks(nodes, slots, source, vblock, tags, integrals, coeffs, recv, recv_tags,
                     half, send_sem, recv_sem, tag_send, tag_recv, own_sem):
    me = lax.axis_index("aux")
    barrier = pltpu.get_barrier_semaphore()

    @pl.loop(1, nodes)
    def _(k):
        pl.semaphore_signal(
            barrier, inc=1, device_id={"aux": lax.rem(me + k, nodes)}, device_id_type=MESH
        )

    def fill(peer):
        for s in range(slots):
            block = integrals[source[peer, s]]
            panel = coeffs[vblock[peer, s]]
            aux_width, size, inner = block.shape
            out = jnp.dot(
                block.reshape(aux_width * size, inner), panel, preferred_element_type=jnp.float32
            )
            half[peer, s] = out.astype(jnp.bfloat16).reshape(aux_width, size, panel.shape[1])

    def peer_of(i):
        pair = i // 2
        flips = (1 - i % 2) * (nodes // 2) + pair % 2 * (nodes // 4)
        flips = flips + (nodes // 4 - pair // 2) % (nodes // 4)
        peer, bit = 0, 1
        while bit < nodes:
            peer = peer + (me // bit + flips // bit) % 2 * bit
            bit *= 2
        return peer

    def copies(peer, landed):
        data = pltpu.make_async_remote_copy(
            src_ref=half.at[peer], dst_ref=recv.at[me], send_sem=send_sem.at[peer],
            recv_sem=recv_sem.at[landed], device_id={"aux": peer}, device_id_type=MESH,
        )
        tag = pltpu.make_async_remote_copy(
            src_ref=tags.at[peer], dst_ref=recv_tags.at[me], send_sem=tag_send.at[peer],
            recv_sem=tag_recv.at[landed], device_id={"aux": peer}, device_id_type=MESH,
        )
        return data, tag

    def send(i):
        peer = peer_of(i)
        fill(peer)
        post(peer)

    def post(peer):
        data, tag = copies(peer, me)
        data.start()
        tag.start()

    fill(peer_of(0))
    pl.semaphore_wait(barrier, nodes - 1)
    post(peer_of(0))
    fill(me)
    own = pltpu.make_async_copy(half.at[me], recv.at[me], own_sem.at[0])
    own_tag = pltpu.make_async_copy(tags.at[me], recv_tags.at[me], own_sem.at[1])
    own.start()
    own_tag.start()

    @pl.loop(2, nodes)
    def _(i):
        send(i)

    own.wait()
    own_tag.wait()

    @pl.loop(1, nodes)
    def _(k):
        peer = lax.rem(me + k, nodes)
        data, tag = copies(peer, peer)
        data.wait()
        tag.wait()


def gram(scale, slots, tags, recv, out, total, fitted, head, following, count, distinct, rows):
    nodes, _, aux_width, size, occ = recv.shape
    groups = out.shape[0] // size
    owned = distinct.shape[0]
    out[...] = jnp.zeros_like(out)

    @pl.loop(0, owned)
    def _(a):
        distinct[a] = 0
        for u in range(groups):
            count[a * groups + u] = 0
            head[a * groups + u] = 0
            rows[a * groups + u] = 0

    @pl.loop(0, nodes)
    def _(node):
        for s in range(slots):
            a = tags[node, 2 * s]
            u = tags[node, 2 * s + 1]

            @pl.when(u >= 0)
            def _():
                item = node * slots + s
                segment = a * groups + u
                seen = count[segment]

                @pl.when(seen == 0)
                def _():
                    rows[a * groups + distinct[a]] = u
                    distinct[a] = distinct[a] + 1

                following[item] = head[segment]
                head[segment] = item
                count[segment] = seen + 1

    def panel(which):
        node, s = which // slots, which % slots
        return jnp.concatenate([recv[node, s, p] for p in range(aux_width)], axis=1)

    def span(u):
        return pl.ds(pl.multiple_of(u * size, size), size)

    @pl.loop(0, owned)
    def _(a):
        present = distinct[a]
        base = a * groups
        first, second = rows[base], rows[base + 1]
        once = (count[base + first] == 1) & ((present < 2) | (count[base + second] == 1))
        simple = once & (present < 3)

        @pl.when(simple & (present == 1))
        def _():
            x = panel(head[base + first])
            out[span(first), span(first)] += lax.dot_general(
                x, x, NT, preferred_element_type=jnp.float32
            )

        @pl.when(simple & (present == 2))
        def _():
            x = jnp.concatenate(
                [panel(head[base + first]), panel(head[base + second])], axis=0
            )
            product = lax.dot_general(x, x, NT, preferred_element_type=jnp.float32)
            out[span(first), span(first)] += product[:size, :size]
            out[span(first), span(second)] += product[:size, size:]
            out[span(second), span(first)] += product[size:, :size]
            out[span(second), span(second)] += product[size:, size:]

        @pl.when((present > 0) & jnp.logical_not(simple))
        def _():
            @pl.loop(0, present)
            def _(i):
                segment = base + rows[base + i]
                item = head[segment]
                members = count[segment]

                @pl.when(members == 1)
                def _():
                    fitted[span(i), :] = panel(item)

                @pl.when(members > 1)
                def _():
                    total[...] = panel(item).astype(jnp.float32)

                    def add(_, item):
                        total[...] += panel(item).astype(jnp.float32)
                        return following[item]

                    lax.fori_loop(1, members, add, following[item])
                    fitted[span(i), :] = total[...].astype(jnp.bfloat16)

            for k in range(1, groups + 1):
                @pl.when(present == k)
                def _():
                    for low in range(0, k, 2):
                        high = min(low + 2, k)
                        product = lax.dot_general(
                            fitted[low * size : high * size, :], fitted[: k * size, :], NT,
                            preferred_element_type=jnp.float32,
                        )
                        for i in range(low, high):
                            for j in range(k):
                                out[span(rows[base + i]), span(rows[base + j])] += product[
                                    (i - low) * size : (i - low + 1) * size,
                                    j * size : (j + 1) * size,
                                ]

    out[...] = out[...] * scale


def exchange(buf, cols, dims, name, coords, sizes, rank_of, landing, send_sem, recv_sem):
    at = dims.index(name)
    found = []
    for step in range(1, sizes[name]):
        other = lax.rem(coords[name] + step, sizes[name])
        target = dict(coords)
        target[name] = other
        pick = (slice(None),) * at + (other,) + (slice(None),) * (len(dims) - at - 1)
        found.append(
            pltpu.make_async_remote_copy(
                src_ref=buf.at[pick + (slice(None), cols)], dst_ref=landing.at[step - 1],
                send_sem=send_sem.at[step - 1], recv_sem=recv_sem.at[step - 1],
                device_id={"aux": rank_of(target)}, device_id_type=MESH,
            )
        )
    return found


def gathered(buf, cols, dims, name, coords, landing, copies):
    at = dims.index(name)
    pick = (slice(None),) * at + (coords[name],) + (slice(None),) * (len(dims) - at - 1)
    value = buf[pick + (slice(None), cols)]
    for step, copy in enumerate(copies):
        copy.wait()
        value = value + landing[step]
    return value


ORDERS = (("x", "y", "z"), ("y", "z", "x"), ("z", "x", "y"))


def scatter_sum(sizes, starts, *refs):
    own, out = refs[:2]
    lands = refs[2:14]
    held = refs[14:23]
    send_sem, recv_sem = refs[23:]
    me = lax.axis_index("aux")
    names = ("z", "y", "x", "c")
    coords = {
        "c": me % 2, "x": me // 2 % 2, "y": me // 4 % 2, "z": me // 8,
    }

    def rank_of(c):
        return ((c["z"] * sizes["y"] + c["y"]) * sizes["x"] + c["x"]) * sizes["c"] + c["c"]

    barrier = pltpu.get_barrier_semaphore()
    partners = 0
    for name in names:
        for step in range(1, sizes[name]):
            target = dict(coords)
            target[name] = lax.rem(coords[name] + step, sizes[name])
            pl.semaphore_signal(
                barrier, inc=1, device_id={"aux": rank_of(target)}, device_id_type=MESH
            )
            partners += 1
    pl.semaphore_wait(barrier, partners)

    orders = [("c",) + order for order in ORDERS]
    bufs = [own] * 3
    left = [list(names) for _ in range(3)]
    spans = [pl.ds(starts[p], starts[p + 1] - starts[p]) for p in range(3)]

    def start(p, stage):
        cols = spans[p] if stage == 0 else slice(None)
        lane = stage * 3 + p
        copies = exchange(bufs[p], cols, left[p], orders[p][stage], coords, sizes, rank_of,
                          lands[lane], send_sem.at[lane], recv_sem.at[lane])
        for copy in copies:
            copy.start()
        return cols, copies

    running = [start(p, 0) for p in range(3)]
    for stage in range(4):
        for p in range(3):
            cols, copies = running[p]
            value = gathered(bufs[p], cols, left[p], orders[p][stage], coords,
                             lands[stage * 3 + p], copies)
            if stage == 3:
                out[:, spans[p]] = value
                continue
            bufs[p] = held[stage * 3 + p]
            bufs[p][...] = value
            left[p].remove(orders[p][stage])
            running[p] = start(p, stage + 1)


def reduce_scatter(matrix, nodes):
    rows, columns = matrix.shape
    sizes = {"z": nodes // 8, "y": 2, "x": 2, "c": 2}
    height = rows // nodes
    starts = (0, columns // 2, columns // 6 * 5, columns)
    deepest = max(sizes["z"] - 1, 1)
    lands, held = [], []
    for stage in range(4):
        for p in range(3):
            done = ("c",) + ORDERS[p][:stage]
            rest = tuple(sizes[d] for d in ("z", "y", "x") if d not in done)
            shape = rest + (height, starts[p + 1] - starts[p])
            axis = done[-1]
            lands.append(pltpu.VMEM((sizes[axis] - 1,) + shape, jnp.float32))
            if stage < 3:
                held.append(pltpu.VMEM(shape, jnp.float32))
    return pl.pallas_call(
        functools.partial(scatter_sum, sizes, starts),
        out_shape=jax.ShapeDtypeStruct((height, columns), jnp.float32),
        in_specs=[pl.BlockSpec(memory_space=pltpu.VMEM)],
        out_specs=pl.BlockSpec(memory_space=pltpu.VMEM),
        scratch_shapes=[
            *lands,
            *held,
            pltpu.SemaphoreType.DMA((12, deepest)),
            pltpu.SemaphoreType.DMA((12, deepest)),
        ],
        compiler_params=pltpu.CompilerParams(
            collective_id=1, has_side_effects=True, vmem_limit_bytes=40 * 2**20
        ),
    )(matrix.reshape(sizes["z"], 2, 2, 2, height, columns))


def fused_body(integrals, block_list, block_count, coeffs):
    stored, aux_width, size, _ = integrals.shape
    basis, occ = coeffs.shape
    nodes = lax.axis_size("aux")
    owned = AUX_DEV // aux_width
    slots = max(2, 64 // nodes)
    positions = jnp.arange(stored, dtype=jnp.int32)
    slab = lax.div(block_list[:, 0], jnp.int32(owned))
    owner = jnp.where(positions < block_count[0], slab, nodes)
    before = (owner[:, None] == owner[None, :]) & (positions[None, :] < positions[:, None])
    target = owner * slots + jnp.sum(before.astype(jnp.int32), axis=1)
    chosen = (target[None, :] == jnp.arange(nodes * slots, dtype=jnp.int32)[:, None]).astype(
        jnp.int32
    )
    fields = jnp.stack(
        [positions, block_list[:, 2], block_list[:, 0] - slab * owned, block_list[:, 1] + 1], axis=0
    )
    picked = jnp.sum(chosen[None] * fields[:, None, :], axis=2)
    source = picked[0].reshape(nodes, slots)
    vblock = picked[1].reshape(nodes, slots)
    tags = jnp.stack([picked[2], picked[3] - 1], axis=1).reshape(nodes, 1, 2 * slots)
    tags = jnp.pad(tags, ((0, 0), (0, 0), (0, 128 - 2 * slots)))
    vmem = pl.BlockSpec(memory_space=pltpu.VMEM)
    smem = pl.BlockSpec(memory_space=pltpu.SMEM)
    recv, recv_tags = pl.pallas_call(
        functools.partial(send_half_blocks, nodes, slots),
        out_shape=(
            jax.ShapeDtypeStruct((nodes, slots, aux_width, size, occ), jnp.bfloat16),
            jax.ShapeDtypeStruct((nodes, 1, 128), jnp.int32),
        ),
        in_specs=[smem, smem, vmem, vmem, vmem],
        out_specs=(pl.BlockSpec(memory_space=pl.ANY), vmem),
        scratch_shapes=[
            pltpu.VMEM((nodes, slots, aux_width, size, occ), jnp.bfloat16),
            pltpu.SemaphoreType.DMA((nodes,)),
            pltpu.SemaphoreType.DMA((nodes,)),
            pltpu.SemaphoreType.DMA((nodes,)),
            pltpu.SemaphoreType.DMA((nodes,)),
            pltpu.SemaphoreType.DMA((2,)),
        ],
        compiler_params=pltpu.CompilerParams(
            collective_id=0, has_side_effects=True, vmem_limit_bytes=40 * 2**20
        ),
    )(source, vblock, tags, integrals, coeffs.reshape(basis // size, size, occ))
    matrix = pl.pallas_call(
        functools.partial(gram, 1.0 / (AUX_DEV * nodes * OCC), slots),
        out_shape=jax.ShapeDtypeStruct((basis, basis), jnp.float32),
        in_specs=[smem, vmem],
        out_specs=vmem,
        scratch_shapes=[
            pltpu.VMEM((size, aux_width * occ), jnp.float32),
            pltpu.VMEM((basis, aux_width * occ), jnp.bfloat16),
            pltpu.SMEM((owned * (basis // size),), jnp.int32),
            pltpu.SMEM((nodes * slots,), jnp.int32),
            pltpu.SMEM((owned * (basis // size),), jnp.int32),
            pltpu.SMEM((owned,), jnp.int32),
            pltpu.SMEM((owned * (basis // size),), jnp.int32),
        ],
        compiler_params=pltpu.CompilerParams(vmem_limit_bytes=40 * 2**20),
    )(recv_tags.reshape(nodes, 128), recv)
    return reduce_scatter(matrix, nodes)


def body(integrals, block_list, block_count, coeffs):
    stored, aux_width, block_size, _ = integrals.shape
    basis, occ_local = coeffs.shape
    basis_blocks = basis // block_size
    aux_nodes = lax.axis_size("aux")
    owned_blocks = AUX_DEV // aux_width
    slot_count = max(2, 64 // aux_nodes)
    segments = owned_blocks * basis_blocks
    coef_blocks = coeffs.reshape(basis_blocks, block_size, occ_local)
    positions = jnp.arange(stored, dtype=jnp.int32)
    is_live = positions < block_count[0]
    owner_slab = jnp.where(is_live, block_list[:, 0] // owned_blocks, aux_nodes)
    member = (owner_slab[:, None] == jnp.arange(aux_nodes, dtype=jnp.int32)[None, :]).astype(
        jnp.int32
    )
    earlier = jnp.cumsum(member, axis=0) - member
    placed = jnp.sum(earlier * member, axis=1)
    target = jnp.where(is_live, owner_slab * slot_count + placed, aux_nodes * slot_count)
    source = (
        jnp.full((aux_nodes * slot_count + 1,), stored, jnp.int32)
        .at[target]
        .set(positions)[: aux_nodes * slot_count]
    )
    blank_tag = jnp.full((1, 3), -1, jnp.int32)
    send_tags = jnp.concatenate([block_list, blank_tag], axis=0)[source].reshape(
        aux_nodes, slot_count, 3
    )
    recv_tags = lax.all_to_all(send_tags, "aux", split_axis=0, concat_axis=0, tiled=True).reshape(
        aux_nodes * slot_count, 3
    )
    filled = recv_tags[:, 1] >= 0
    seg_of = jnp.where(
        filled, recv_tags[:, 1] * owned_blocks + recv_tags[:, 0] % owned_blocks, segments
    )
    seg_table = (jnp.arange(segments, dtype=jnp.int32)[:, None] == seg_of[None, :]).astype(
        jnp.bfloat16
    )
    padded = jnp.concatenate(
        [integrals, jnp.zeros((1,) + integrals.shape[1:], jnp.bfloat16)], axis=0
    )
    outgoing = padded[source].reshape(aux_nodes, slot_count, aux_width, block_size, block_size)
    lam_index = jnp.where(filled, recv_tags[:, 2], 0)
    recv_coef = coef_blocks[lam_index]
    item_block = lax.all_to_all(outgoing, "aux", split_axis=0, concat_axis=0, tiled=True)
    item_count = item_block.shape[2]
    flat_ints = item_block.reshape(aux_nodes * slot_count, item_count, block_size, block_size)
    half_rows = lax.dot_general(
        flat_ints, recv_coef, (((3,), (1,)), ((0,), (0,))), preferred_element_type=jnp.float32
    ).astype(jnp.bfloat16)
    summed = jnp.dot(
        seg_table, half_rows.reshape(aux_nodes * slot_count, -1), preferred_element_type=jnp.float32
    )
    fitted = summed.reshape(segments, item_count, block_size, occ_local)
    fitted = fitted.astype(jnp.bfloat16).reshape(
        basis_blocks, owned_blocks, aux_width, block_size, occ_local
    )
    fitted = fitted.transpose(0, 3, 1, 2, 4).reshape(basis, owned_blocks * aux_width * occ_local)
    scale_factor = 1.0 / (AUX_DEV * aux_nodes * OCC)
    return lax.psum_scatter(
        lax.dot_general(
            fitted, fitted, (((1,), (1,)), ((), ())), preferred_element_type=jnp.float32
        )
        * scale_factor,
        ("aux", "occ"),
        scatter_dimension=0,
        tiled=True,
    )


def solution(mesh):
    placed = (
        P(("frag", "aux"), None, None, None),
        P(("frag", "aux"), None),
        P(("frag", "aux")),
        P("frag", "occ"),
    )
    simple = mesh.shape["occ"] == 1 and mesh.shape["aux"] in (8, 16, 32, 64)
    return jax.shard_map(
        fused_body if simple else body, mesh=mesh, in_specs=placed, out_specs=P(("frag", "aux", "occ"), None), check_vma=False
    )
```
